32 devices in a mesh: group: 2 (over y), gx: 4 (over z), gy: 2 (over x), gz: 2 (over core).
Axes of the slice: x: 2, y: 2, z: 4, core: 2. Of those that a mesh axis runs over, the one named last changes fastest.
Arguments:
- board_temp: float32 [32, 256, 1024], P('group', 'gx', ('gy', 'gz')), parts along dimension 0, may hold values from -4 to 4
- board_coeff: float32 [32, 256, 1024], P('group', 'gx', ('gy', 'gz')), parts along dimension 0, may hold values from 0.03 to 0.12
- source: float32 [512, 1024], P(('group', 'gx'), ('gy', 'gz')), parts along dimension 0, may hold values from -4 to 4
- board_target: float32 [32, 256, 1024], P('group', 'gx', ('gy', 'gz')), parts along dimension 0, may hold values from -4 to 4
- pipe_temp: float32 [896, 2048], P(('group', 'gy', 'gz'), 'gx'), parts along dimension 0, may hold values from -4 to 4
- pipe_target: float32 [896, 2048], P(('group', 'gy', 'gz'), 'gx'), parts along dimension 0, may hold values from -4 to 4
- pipe_cond: float32 [896], P(('group', 'gy', 'gz')), parts along dimension 0, may hold values from 0.1 to 0.45
- contact_gain: float32 [896], P(('group', 'gy', 'gz')), parts along dimension 0, may hold values from 0.1 to 0.4
- contact_col: int32 [896, 2048], P(('group', 'gy', 'gz'), 'gx'), parts along dimension 0, may hold values from 0 to 255
- pipe_owner: int32 [896], P(('group', 'gy', 'gz')), parts along dimension 0, may hold values from 0 to 3, as said below
- step_index: int32 [2], P('group'), parts along dimension 0, may hold values from 0 to 99999
Outputs:
- board_adjoint: float32 [32, 256, 1024], P('group', 'gx', ('gy', 'gz')), parts along dimension 0
- pipe_adjoint: float32 [896, 2048], P(('group', 'gy', 'gz'), 'gx'), parts along dimension 0
- source_gradient: float32 [512, 1024], P(('group', 'gx'), ('gy', 'gz')), parts along dimension 0
The draws below stay inside these ranges and needn't reach their ends.
There are 2 independent parts, one for each index of `group`. The reference program is written for one: setup_inputs(seed, part) draws one part's arguments, and reference() takes and returns one part's arrays. A program takes and returns all parts, laid end to end along the dimension named above; each array names one. Nothing has to cross between parts.
Inputs may be any that keep to these rules, and one draw needn't show every extreme that they name: `pipe_owner`: in each aligned block of 112 pipes one strip, the same in every block, has exactly 28 of the block's pipes, and no strip has more than 28 of them.
All inputs are finite; a program needn't handle non-finite values.
Results may differ from the reference program's by a relative error of at most 0.0003.
Values sent between devices are 32-bit elements; how exact they have to be, the bound alone decides.
A program may use at most 64 MiB of HBM per device.

```python
import math
import jax
import jax.numpy as jnp

LAYERS = 16
CY = 256
NODES = 2048
PIPE_DEV = 112
OWNERS = 4
PIPES = 448
CAP = 28
NX = 256
NY = 1024


def draw_pipe_owner(key, part):
    key = jax.random.fold_in(key, 7)
    heavy_key, order_key, shift_key = jax.random.split(key, 3)
    blocks = PIPES // PIPE_DEV
    heavy = jax.random.randint(heavy_key, (), 0, OWNERS)
    ranking = jax.vmap(lambda one_key: jax.random.permutation(one_key, PIPE_DEV))(jax.random.split(order_key, blocks))
    shifts = jax.random.randint(shift_key, (blocks, 1), 0, OWNERS - 1)
    others = (ranking - CAP + shifts) % (OWNERS - 1)
    picked = jnp.where(ranking < CAP, heavy, (heavy + 1 + others) % OWNERS)
    return picked.reshape(PIPES).astype(jnp.int32)


def plant(values, stream_key, least, largest):
    longest = values.shape.index(max(values.shape))
    spots = []
    for shift in (0, 1):
        where = [jax.random.randint(jax.random.fold_in(stream_key, axis), (), 0, length) for axis, length in enumerate(values.shape)]
        where[longest] = (where[longest] + shift) % values.shape[longest]
        spots.append(tuple(where))
    return values.at[spots[0]].set(least).at[spots[1]].set(largest)


def shard_levels(rng, shape, shards, low, largest):
    def one(dim, shards_of):
        steps = jax.random.uniform(jax.random.fold_in(jax.random.fold_in(rng, 6), dim), (shards_of,), jnp.float32, low / len(shards), largest / len(shards))
        return jnp.repeat(jnp.exp(steps), shape[dim] // shards_of).reshape((-1,) + (1,) * (len(shape) - dim - 1))

    level = one(*shards[0])
    for cut in shards[1:]:
        level = level * one(*cut)
    return level


def normal_values(rng, shape, scale, most, shards=(), kind=jnp.bfloat16):
    result = scale * jax.random.normal(rng, shape, jnp.float32)
    if shards:
        result = result * shard_levels(rng, shape, shards, -0.22, 0.18)
    return jnp.clip(result, -most, most).astype(kind)


def setup_inputs(seed: int = 0, part: int = 0) -> dict:
    key_of = jax.random.split(jax.random.key(seed), 12)
    own_keys = jax.random.split(jax.random.fold_in(key_of[11], part), 12)
    return {
        "board_temp": normal_values(own_keys[0], (LAYERS, NX, NY), 1.0, 4.0, ((1, 4), (2, 4)), jnp.float32),
        "board_coeff": jnp.clip(jnp.exp(math.log(0.12) - 1.3862944 * jax.random.uniform(own_keys[1], (LAYERS, NX, NY), jnp.float32) ** shard_levels(own_keys[1], (LAYERS, NX, NY), ((1, 4), (2, 4)), -0.2, 0.2)), 0.03, 0.12),
        "source": normal_values(own_keys[2], (NX, NY), 1.0, 4.0, ((0, 4), (1, 4)), jnp.float32),
        "board_target": normal_values(own_keys[3], (LAYERS, NX, NY), 1.0, 4.0, ((1, 4), (2, 4)), jnp.float32),
        "pipe_temp": normal_values(own_keys[4], (PIPES, NODES), 1.0, 4.0, ((0, 4), (1, 4)), jnp.float32),
        "pipe_target": normal_values(own_keys[5], (PIPES, NODES), 1.0, 4.0, ((0, 4), (1, 4)), jnp.float32),
        "pipe_cond": jnp.clip(0.1 + 0.35 * jax.random.uniform(own_keys[6], (PIPES,), jnp.float32) ** shard_levels(own_keys[6], (PIPES,), ((0, 4),), -0.2, 0.2), 0.1, 0.45),
        "contact_gain": jnp.clip(jnp.exp(math.log(0.4) - 1.3862944 * jax.random.uniform(own_keys[7], (PIPES,), jnp.float32) ** shard_levels(own_keys[7], (PIPES,), ((0, 4),), -0.2, 0.2)), 0.1, 0.4),
        "contact_col": plant(jax.random.randint(own_keys[8], (PIPES, NODES), 0, CY), jax.random.fold_in(own_keys[8], 1), 0, CY - 1).astype(jnp.int32),
        "pipe_owner": draw_pipe_owner(jax.random.fold_in(jax.random.fold_in(key_of[11], part), 71), part),
        "step_index": jax.random.randint(own_keys[10], (1,), 0, 100000).astype(jnp.int32),
    }


CUBIC_TERM = 0.05
BOARD_SHARE = 0.5
PIPE_SHARE = 1.0
VERTICAL = 1.0
PERIOD_STEPS = 24.0


def lap_board(field):
    padded = jnp.pad(field, 1)
    lateral = padded[1:-1, 2:, 1:-1] + padded[1:-1, :-2, 1:-1] + padded[1:-1, 1:-1, 2:] + padded[1:-1, 1:-1, :-2] - 4.0 * field
    across = padded[2:, 1:-1, 1:-1] + padded[:-2, 1:-1, 1:-1] - 2.0 * field
    return lateral + VERTICAL * across


def lap_chain(field):
    edge = jnp.zeros_like(field[:, :1])
    right = jnp.concatenate([field[:, 1:] - field[:, :-1], edge], axis=1)
    left = jnp.concatenate([edge, field[:, :-1] - field[:, 1:]], axis=1)
    return right + left


def power(step):
    return 1.0 + 0.5 * jnp.sin((2.0 * math.pi / PERIOD_STEPS) * step.astype(jnp.float32))


def reference(board_temp, board_coeff, source, board_target, pipe_temp, pipe_target, pipe_cond, contact_gain, contact_col, pipe_owner, step_index):
    node_rows = (jnp.arange(NODES, dtype=jnp.int32) * NX) // NODES
    columns = pipe_owner[:, None] * CY + contact_col
    row_grid = jnp.broadcast_to(node_rows[None, :], columns.shape)
    gain = contact_gain[:, None]
    conduct = pipe_cond[:, None]

    def spread(values):
        return jnp.zeros((NX, NY), jnp.float32).at[row_grid, columns].add(values)

    def forward(board, pipes, moment):
        differ = pipes - board[0][row_grid, columns]
        flux = gain * (differ + CUBIC_TERM * differ * differ * differ)
        board_next = board + board_coeff * lap_board(board)
        upper = board_next[0] + power(moment) * source + BOARD_SHARE * spread(flux)
        board_next = board_next.at[0].set(upper)
        pipe_next = pipes + conduct * lap_chain(pipes) - PIPE_SHARE * flux
        return board_next, pipe_next, differ

    def backward(board_adj, pipe_adj, differ):
        weight = gain * (1.0 + 3.0 * CUBIC_TERM * differ * differ)
        sensed = (BOARD_SHARE * board_adj[0][row_grid, columns] - PIPE_SHARE * pipe_adj) * weight
        board_prev = board_adj + lap_board(board_coeff * board_adj)
        board_prev = board_prev.at[0].add(-spread(sensed))
        pipe_prev = pipe_adj + conduct * lap_chain(pipe_adj) + sensed
        return board_prev, pipe_prev

    start = step_index[0]
    board_one, pipe_one, differ_zero = forward(board_temp, pipe_temp, start)
    board_two, pipe_two, differ_one = forward(board_one, pipe_one, start + 1)
    seed_board = board_two - board_target
    seed_pipe = pipe_two - pipe_target
    adj_board_one, adj_pipe_one = backward(seed_board, seed_pipe, differ_one)
    board_adjoint, pipe_adjoint = backward(adj_board_one, adj_pipe_one, differ_zero)
    source_gradient = power(start + 1) * seed_board[0] + power(start) * adj_board_one[0]
    return board_adjoint, pipe_adjoint, source_gradient
```

```python
import functools
import math

import jax
import jax.numpy as jnp
from jax import lax
from jax.experimental import pallas as pl
from jax.experimental.pallas import tpu as pltpu
from jax.sharding import PartitionSpec as P

CUBIC_TERM = 0.05
BOARD_SHARE = 0.5
PERIOD_STEPS = 24.0
SLOTS = 32
LOW = 16
LANES = 128
EXACT = lax.Precision.HIGHEST
MESH = pl.DeviceIdType.MESH
F32 = jnp.float32


def power(moment):
    return 1.0 + 0.5 * jnp.sin(2.0 * math.pi / PERIOD_STEPS * moment.astype(F32))


def kernel(
    sizes,
    board,
    coeff,
    source,
    target,
    pipe_temp,
    pipe_target,
    contact,
    owner,
    traits,
    powers,
    board_out,
    pipe_out,
    grad_out,
    x,
    y,
    e,
    perm,
    send_a,
    send_b,
    recv_a,
    recv_b,
    send_c,
    recv_c,
    turned,
    pipes,
    wanted,
    high_part,
    low_part,
    flux,
    column,
    cells_hot,
    differ,
    sums,
    row_send,
    row_recv,
    col_send,
    col_recv,
    end_send,
    end_recv,
    pipe_sems,
    row_sems,
    col_sems,
    end_sems,
):
    gx_count, gz_count, owners = sizes
    layers, rows, cols = board.shape
    pipe_count, nodes = pipe_temp.shape
    per_row = nodes // rows
    slots = owners * SLOTS
    blocks = slots // LANES
    highs = cols // LOW
    gx = lax.axis_index("gx")
    strip = lax.axis_index("gy") * gz_count + lax.axis_index("gz")
    has = (gx > 0, gx < gx_count - 1, strip > 0, strip < owners - 1)

    def at_strip(other):
        return {"gy": other // gz_count, "gz": lax.rem(other, gz_count)}

    gx_near = ({"gx": gx - 1}, {"gx": gx + 1})
    strip_near = (at_strip(strip - 1), at_strip(strip + 1))

    barrier = pltpu.get_barrier_semaphore()
    for side in range(2):

        @pl.when(has[side])
        def _():
            pl.semaphore_signal(barrier, inc=1, device_id=gx_near[side], device_id_type=MESH)

    for d in range(1, owners):
        pl.semaphore_signal(
            barrier, inc=1, device_id=at_strip(lax.rem(strip + d, owners)), device_id_type=MESH
        )

    def halo_copy(send, recv, sems, moment, side, near):
        return pltpu.make_async_remote_copy(
            src_ref=send.at[moment, side],
            dst_ref=recv.at[moment, 1 - side],
            send_sem=sems.at[0, moment, side],
            recv_sem=sems.at[1, moment, 1 - side],
            device_id=near[side],
            device_id_type=MESH,
        )

    def arrival(send, recv, sems, moment, side, near):
        return pltpu.make_async_remote_copy(
            src_ref=send.at[moment, side],
            dst_ref=recv.at[moment, side],
            send_sem=sems.at[0, moment, side],
            recv_sem=sems.at[1, moment, side],
            device_id=near[side],
            device_id_type=MESH,
        )

    board_kinds = (
        (row_send, row_recv, row_sems, gx_near, 0),
        (col_send, col_recv, col_sems, strip_near, 2),
    )
    end_kind = ((end_send, end_recv, end_sems, gx_near, 0),)

    def start(kinds, moment):
        for send, recv, sems, near, base in kinds:
            for side in range(2):

                @pl.when(has[base + side])
                def _():
                    halo_copy(send, recv, sems, moment, side, near).start()

    def await_halo(kinds, moment):
        for send, recv, sems, near, base in kinds:
            for side in range(2):

                @pl.when(has[base + side])
                def _():
                    arrival(send, recv, sems, moment, side, near).wait_recv()

    def await_sent(kinds, moment):
        for send, recv, sems, near, base in kinds:
            for side in range(2):

                @pl.when(has[base + side])
                def _():
                    halo_copy(send, recv, sems, moment, side, near).wait_send()

    for send, recv, sems, near, base in board_kinds:
        for side in range(2):

            @pl.when(jnp.logical_not(has[base + side]))
            def _():
                for moment in range(4):
                    recv[moment, side] = jnp.zeros(recv.shape[2:], F32)

    lane_cols = lax.broadcasted_iota(jnp.int32, (rows, cols), 1)
    row_ids = lax.broadcasted_iota(jnp.int32, (rows, cols), 0)
    lane_one = lax.broadcasted_iota(jnp.int32, (rows, LANES), 1)
    end_rows = lax.broadcasted_iota(jnp.int32, (rows, slots), 0)

    def boundary(field, moment):
        def body(layer, carry):
            low, high = carry
            now = field[layer + 1]
            row_send[moment, 0, pl.ds(layer, 1), :] = now[0:1, :]
            row_send[moment, 1, pl.ds(layer, 1), :] = now[rows - 1 : rows, :]
            mine = lane_one == layer
            low = jnp.where(mine, now[:, 0:1], low)
            high = jnp.where(mine, now[:, cols - 1 : cols], high)
            return low, high

        zero = jnp.zeros((rows, LANES), F32)
        low, high = lax.fori_loop(0, layers, body, (zero, zero))
        col_send[moment, 0] = low
        col_send[moment, 1] = high
        start(board_kinds, moment)

    def laplacian(field, moment, put):
        def body(layer, _):
            now = field[layer + 1]
            above = row_recv[moment, 0, pl.ds(layer, 1), :]
            below = row_recv[moment, 1, pl.ds(layer, 1), :]
            before = pltpu.roll(col_recv[moment, 0], lax.rem(LANES - layer, LANES), 1)
            after = pltpu.roll(col_recv[moment, 1], LANES - 1 - layer, 1)
            if cols > LANES:
                before = jnp.concatenate([before, now[:, LANES:]], axis=1)
                after = jnp.concatenate([now[:, : cols - LANES], after], axis=1)
            up = jnp.where(row_ids == 0, above, pltpu.roll(now, 1, 0))
            down = jnp.where(row_ids == rows - 1, below, pltpu.roll(now, rows - 1, 0))
            left = jnp.where(lane_cols == 0, before, pltpu.roll(now, 1, 1))
            right = jnp.where(lane_cols == cols - 1, after, pltpu.roll(now, cols - 1, 1))
            put(layer, now, (up + down + left + right + field[layer] + field[layer + 2]) - 6.0 * now)
            return 0

        lax.fori_loop(0, layers, body, 0)

    zero_layer = jnp.zeros((rows, cols), F32)
    for field in (x, y, e):
        field[0] = zero_layer
        field[layers + 1] = zero_layer
    sums[...] = jnp.zeros(sums.shape, F32)
    x[1 : layers + 1] = board[...]

    own = owner[...]
    strips = -(-owners // 8) * 8
    strip_ids = lax.broadcasted_iota(jnp.int32, (strips, pipe_count), 0)
    hot = jnp.where(strip_ids == own, 1.0, 0.0).astype(F32)
    earlier = jnp.where(
        lax.broadcasted_iota(jnp.int32, (pipe_count, pipe_count), 0)
        < lax.broadcasted_iota(jnp.int32, (pipe_count, pipe_count), 1),
        1.0,
        0.0,
    ).astype(F32)
    ahead = jnp.dot(hot, earlier, preferred_element_type=F32)
    rank = jnp.sum(hot * ahead, axis=0, keepdims=True)
    place = own * SLOTS + rank.astype(jnp.int32)
    slot_ids = lax.broadcasted_iota(jnp.int32, (slots, pipe_count), 0)
    perm[...] = jnp.where(slot_ids == place, 1.0, 0.0).astype(F32)

    def sort(values):
        return jnp.dot(perm[...], values, precision=EXACT, preferred_element_type=F32)

    near_count = jnp.int32(owners - 1)
    near_count = near_count + jnp.where(has[0], 1, 0) + jnp.where(has[1], 1, 0)
    pl.semaphore_wait(barrier, near_count)
    boundary(x, 0)

    def exchange(send, recv, which):
        copies = []
        for d in range(1, owners):
            other = lax.rem(strip + d, owners)
            copies.append(
                pltpu.make_async_remote_copy(
                    src_ref=send.at[pl.ds(pl.multiple_of(other * SLOTS, SLOTS), SLOTS)],
                    dst_ref=recv.at[pl.ds(pl.multiple_of(strip * SLOTS, SLOTS), SLOTS)],
                    send_sem=pipe_sems.at[0, which, d],
                    recv_sem=pipe_sems.at[1, which, d],
                    device_id=at_strip(other),
                    device_id_type=MESH,
                )
            )
        for copy in copies:
            copy.start()
        here = pl.ds(pl.multiple_of(strip * SLOTS, SLOTS), SLOTS)
        recv[here, :] = send[here, :]
        return copies

    def await_pipes(recv, send, which):
        for d in range(1, owners):
            source_strip = lax.rem(strip + owners - d, owners)
            pltpu.make_async_remote_copy(
                src_ref=send.at[pl.ds(pl.multiple_of(source_strip * SLOTS, SLOTS), SLOTS)],
                dst_ref=recv.at[pl.ds(pl.multiple_of(source_strip * SLOTS, SLOTS), SLOTS)],
                send_sem=pipe_sems.at[0, which, d],
                recv_sem=pipe_sems.at[1, which, d],
                device_id=at_strip(source_strip),
                device_id_type=MESH,
            ).wait_recv()

    send_a[:, 0:nodes] = sort(pipe_temp[...])
    send_a[:, nodes : 2 * nodes] = jnp.dot(
        perm[...], contact[...].astype(F32), preferred_element_type=F32
    )
    send_a[:, 2 * nodes :] = sort(traits[...])
    copies_a = exchange(send_a, recv_a, 0)
    send_b[...] = sort(pipe_target[...])
    copies_b = exchange(send_b, recv_b, 1)

    def forward_put(to):
        def put(layer, now, lap):
            to[layer + 1] = now + coeff[layer] * lap

        return put

    await_halo(board_kinds, 0)
    laplacian(x, 0, forward_put(y))

    def turn(recv, first, put):
        for b in range(blocks):
            turned[...] = recv[b * LANES : (b + 1) * LANES, first : first + nodes].T
            for k in range(per_row):
                if per_row == 1:
                    values = turned[...]
                else:
                    values = turned[pl.ds(k, rows, stride=per_row), :]
                put(k, b, values)

    def put_pipes(k, b, values):
        pipes[k, :, b * LANES : (b + 1) * LANES] = values

    def put_wanted(k, b, values):
        wanted[k, :, b * LANES : (b + 1) * LANES] = values

    def put_column(k, b, values):
        column[k, :, b * LANES : (b + 1) * LANES] = values.astype(jnp.int32)

    await_pipes(recv_a, send_a, 0)
    turn(recv_a, 0, put_pipes)

    def send_ends(moment):
        first = pipes[0, 0:8, :]
        last = pipes[per_row - 1, rows - 8 : rows, :]
        end_send[moment, 0] = first
        end_send[moment, 1] = last
        start(end_kind, moment)

    send_ends(0)
    turn(recv_a, nodes, put_column)
    trait_rows = [
        recv_a[b * LANES : (b + 1) * LANES, 2 * nodes : 2 * nodes + LANES].T[0:8, :]
        for b in range(blocks)
    ]
    trait_rows = jnp.concatenate(trait_rows, axis=1) if blocks > 1 else trait_rows[0]
    gain = trait_rows[0:1, :]
    conduct = trait_rows[1:2, :]

    low_ids = lax.broadcasted_iota(jnp.int32, (LOW, slots), 0)
    high_ids = lax.broadcasted_iota(jnp.int32, (highs, slots), 0)

    def hot_body(row, _):
        for k in range(per_row):
            cell = jnp.bitwise_and(column[k, pl.ds(row, 1), :], LOW - 1)
            cells_hot[row, :, k * slots : (k + 1) * slots] = jnp.where(
                low_ids == cell, 1.0, 0.0
            ).astype(jnp.bfloat16)
        return 0

    lax.fori_loop(0, rows, hot_body, 0)

    def spread():
        high_part[...] = flux[...].astype(jnp.bfloat16).astype(F32)
        low_part[...] = flux[...] - high_part[...]

        def one_row(row):
            parts = []
            for k in range(per_row):
                mine = high_ids == jnp.right_shift(column[k, pl.ds(row, 1), :], 4)
                top = jnp.where(mine, high_part[k, pl.ds(row, 1), :], 0.0)
                rest = jnp.where(mine, low_part[k, pl.ds(row, 1), :], 0.0)
                parts.append(jnp.concatenate([top, rest], axis=0).astype(jnp.bfloat16))
            hot_values = jnp.concatenate(parts, axis=1)
            both = lax.dot_general(
                hot_values,
                cells_hot[row],
                (((1,), (1,)), ((), ())),
                preferred_element_type=F32,
            )
            sums[pl.ds(pl.multiple_of(row * highs, highs), highs), 0:LOW] = both[:highs] + both[highs:]

        def body(step, _):
            for part in range(4):
                one_row(step * 4 + part)
            return 0

        lax.fori_loop(0, rows // 4, body, 0)
        pieces = []
        per_lane = LANES // LOW
        for half in range(cols // LANES):
            total = sums[pl.ds(half * per_lane, rows, stride=highs), :]
            for h in range(1, per_lane):
                total = total + pltpu.roll(
                    sums[pl.ds(half * per_lane + h, rows, stride=highs), :], h * LOW, 1
                )
            pieces.append(total)
        return jnp.concatenate(pieces, axis=1) if len(pieces) > 1 else pieces[0]

    def fetch(field, k):
        out = []
        for b in range(blocks):
            cell = column[k, :, b * LANES : (b + 1) * LANES]
            within = jnp.bitwise_and(cell, LANES - 1)
            which = jnp.right_shift(cell, 7)
            found = None
            for half in range(cols // LANES):
                table = field[1, :, half * LANES : (half + 1) * LANES]
                values = jnp.take_along_axis(table, within, axis=1, mode="promise_in_bounds")
                found = values if found is None else jnp.where(which == half, values, found)
            out.append(found)
        return jnp.concatenate(out, axis=1) if blocks > 1 else out[0]

    def chain_next(moment, sign):
        await_halo(end_kind, moment)
        planes = [pipes[k] for k in range(per_row)]
        first, last = planes[0], planes[-1]
        low = jnp.where(has[0], end_recv[moment, 0, 7:8, :], first[0:1, :])
        high = jnp.where(has[1], end_recv[moment, 1, 0:1, :], last[rows - 1 : rows, :])
        previous = jnp.where(end_rows == 0, low, pltpu.roll(last, 1, 0))
        following = jnp.where(end_rows == rows - 1, high, pltpu.roll(first, rows - 1, 0))
        for k in range(per_row):
            now = planes[k]
            left = planes[k - 1] if k > 0 else previous
            right = planes[k + 1] if k < per_row - 1 else following
            pipes[k] = now + conduct * ((right - now) + (left - now)) + sign * flux[k]

    def couple(field, moment):
        for k in range(per_row):
            apart = pipes[k] - fetch(field, k)
            differ[moment, k] = apart
            flux[k] = gain * (apart + CUBIC_TERM * apart * apart * apart)

    def couple_back(field, moment):
        for k in range(per_row):
            apart = differ[moment, k]
            weight = gain * (1.0 + 3.0 * CUBIC_TERM * apart * apart)
            flux[k] = (BOARD_SHARE * fetch(field, k) - pipes[k]) * weight

    couple(x, 0)
    chain_next(0, -1.0)
    send_ends(1)
    y[1] = y[1] + powers[0:1, :] * source[...] + BOARD_SHARE * spread()
    boundary(y, 1)

    couple(y, 1)
    chain_next(1, -1.0)
    await_pipes(recv_b, send_b, 1)
    turn(recv_b, 0, put_wanted)
    for k in range(per_row):
        pipes[k] = pipes[k] - wanted[k]
    send_ends(2)
    deposit = spread()
    await_halo(board_kinds, 1)

    def seed_put(layer, now, lap):
        x[layer + 1] = now + coeff[layer] * lap - target[layer]

    laplacian(y, 1, seed_put)
    x[1] = x[1] + powers[1:2, :] * source[...] + BOARD_SHARE * deposit
    grad_out[...] = powers[1:2, :] * x[1]

    def weigh(layer, _):
        e[layer + 1] = coeff[layer] * x[layer + 1]
        return 0

    lax.fori_loop(0, layers, weigh, 0)
    boundary(e, 2)

    couple_back(x, 1)
    chain_next(2, 1.0)
    send_ends(3)
    deposit = spread()
    await_halo(board_kinds, 2)

    def back_put(layer, now, lap):
        y[layer + 1] = x[layer + 1] + lap

    laplacian(e, 2, back_put)
    y[1] = y[1] - deposit
    grad_out[...] = grad_out[...] + powers[0:1, :] * y[1]

    def weigh_again(layer, _):
        e[layer + 1] = coeff[layer] * y[layer + 1]
        return 0

    lax.fori_loop(0, layers, weigh_again, 0)
    boundary(e, 3)

    couple_back(y, 0)
    chain_next(3, 1.0)
    for b in range(blocks):
        for k in range(per_row):
            values = pipes[k, :, b * LANES : (b + 1) * LANES]
            if per_row == 1:
                turned[...] = values
            else:
                turned[pl.ds(k, rows, stride=per_row), :] = values
        send_c[b * LANES : (b + 1) * LANES, :] = turned[...].T
    copies_c = exchange(send_c, recv_c, 2)
    deposit = spread()
    await_halo(board_kinds, 3)

    def last_put(layer, now, lap):
        board_out[layer] = y[layer + 1] + lap

    laplacian(e, 3, last_put)
    board_out[0] = board_out[0] - deposit
    await_pipes(recv_c, send_c, 2)
    pipe_out[...] = lax.dot_general(
        perm[...],
        recv_c[...],
        (((0,), (0,)), ((), ())),
        precision=EXACT,
        preferred_element_type=F32,
    )

    for moment in range(4):
        await_sent(board_kinds, moment)
        await_sent(end_kind, moment)
    for copy in copies_a + copies_b + copies_c:
        copy.wait_send()


def solution(mesh):
    gx_count = mesh.shape["gx"]
    gz_count = mesh.shape["gz"]
    owners = mesh.shape["gy"] * gz_count

    def local(
        board_temp,
        board_coeff,
        source,
        board_target,
        pipe_temp,
        pipe_target,
        pipe_cond,
        contact_gain,
        contact_col,
        pipe_owner,
        step_index,
    ):
        layers, rows, cols = board_temp.shape
        pipe_count, nodes = pipe_temp.shape
        per_row = nodes // rows
        slots = owners * SLOTS
        highs = cols // LOW
        traits = jnp.concatenate(
            [
                contact_gain[:, None],
                pipe_cond[:, None],
                jnp.zeros((pipe_count, LANES - 2), F32),
            ],
            axis=1,
        )
        moments = step_index[0] + jnp.arange(2, dtype=jnp.int32)
        powers = jnp.broadcast_to(power(moments)[:, None], (2, cols))
        field = pltpu.VMEM((layers + 2, rows, cols), F32)
        planes = pltpu.VMEM((per_row, rows, slots), F32)
        vmem = pl.BlockSpec(memory_space=pltpu.VMEM)
        return pl.pallas_call(
            functools.partial(kernel, (gx_count, gz_count, owners)),
            out_shape=(
                jax.ShapeDtypeStruct(board_temp.shape, F32),
                jax.ShapeDtypeStruct(pipe_temp.shape, F32),
                jax.ShapeDtypeStruct(source.shape, F32),
            ),
            in_specs=[vmem] * 10,
            out_specs=[vmem] * 3,
            scratch_shapes=[
                field,
                field,
                field,
                pltpu.VMEM((slots, pipe_count), F32),
                pltpu.VMEM((slots, 2 * nodes + LANES), F32),
                pltpu.VMEM((slots, nodes), F32),
                pltpu.VMEM((slots, 2 * nodes + LANES), F32),
                pltpu.VMEM((slots, nodes), F32),
                pltpu.VMEM((slots, nodes), F32),
                pltpu.VMEM((slots, nodes), F32),
                pltpu.VMEM((nodes, LANES), F32),
                planes,
                planes,
                planes,
                planes,
                planes,
                pltpu.VMEM((per_row, rows, slots), jnp.int32),
                pltpu.VMEM((rows, LOW, per_row * slots), jnp.bfloat16),
                pltpu.VMEM((2, per_row, rows, slots), F32),
                pltpu.VMEM((rows * highs, LANES), F32),
                pltpu.VMEM((4, 2, layers, cols), F32),
                pltpu.VMEM((4, 2, layers, cols), F32),
                pltpu.VMEM((4, 2, rows, LANES), F32),
                pltpu.VMEM((4, 2, rows, LANES), F32),
                pltpu.VMEM((4, 2, 8, slots), F32),
                pltpu.VMEM((4, 2, 8, slots), F32),
                pltpu.SemaphoreType.DMA((2, 3, owners)),
                pltpu.SemaphoreType.DMA((2, 4, 2)),
                pltpu.SemaphoreType.DMA((2, 4, 2)),
                pltpu.SemaphoreType.DMA((2, 4, 2)),
            ],
            compiler_params=pltpu.CompilerParams(
                collective_id=0, has_side_effects=True, vmem_limit_bytes=48 * 1024 * 1024
            ),
        )(
            board_temp,
            board_coeff,
            source,
            board_target,
            pipe_temp,
            pipe_target,
            contact_col,
            pipe_owner[None, :],
            traits,
            powers,
        )

    placed = (
        P("group", "gx", ("gy", "gz")),
        P("group", "gx", ("gy", "gz")),
        P(("group", "gx"), ("gy", "gz")),
        P("group", "gx", ("gy", "gz")),
        P(("group", "gy", "gz"), "gx"),
        P(("group", "gy", "gz"), "gx"),
        P(("group", "gy", "gz")),
        P(("group", "gy", "gz")),
        P(("group", "gy", "gz"), "gx"),
        P(("group", "gy", "gz")),
        P("group"),
    )
    return jax.shard_map(
        local,
        mesh=mesh,
        in_specs=placed,
        out_specs=(
            P("group", "gx", ("gy", "gz")),
            P(("group", "gy", "gz"), "gx"),
            P(("group", "gx"), ("gy", "gz")),
        ),
        check_vma=False,
    )
```

```python
import functools
import math

import jax
import jax.numpy as jnp
from jax import lax
from jax.experimental import pallas as pl
from jax.experimental.pallas import tpu as pltpu
from jax.sharding import PartitionSpec as P

CUBIC_TERM = 0.05
BOARD_SHARE = 0.5
PERIOD_STEPS = 24.0
SLOTS = 32
LOW = 16
LANES = 128
EXACT = lax.Precision.HIGHEST
MESH = pl.DeviceIdType.MESH
F32 = jnp.float32


def power(moment):
    return 1.0 + 0.5 * jnp.sin(2.0 * math.pi / PERIOD_STEPS * moment.astype(F32))


def kernel(
    sizes,
    board_hbm,
    coeff_hbm,
    source_hbm,
    target_hbm,
    pipe_temp_hbm,
    pipe_target_hbm,
    contact_hbm,
    owner,
    gains,
    conds,
    powers,
    board_out,
    pipe_out,
    grad_out,
    coeff,
    source,
    target,
    pipe_temp,
    pipe_target,
    contact,
    in_sems,
    trait_send,
    trait_recv,
    x,
    y,
    e,
    perm,
    send_a,
    send_b,
    recv_a,
    recv_b,
    send_c,
    recv_c,
    turned,
    pipes,
    wanted,
    high_part,
    low_part,
    flux,
    column,
    cells_hot,
    differ,
    sums,
    row_send,
    row_recv,
    col_send,
    col_recv,
    end_send,
    end_recv,
    pipe_sems,
    row_sems,
    col_sems,
    end_sems,
):
    gx_count, gz_count, owners = sizes
    layers, rows, cols = board_hbm.shape
    pipe_count, nodes = pipe_temp.shape
    per_row = nodes // rows
    slots = owners * SLOTS
    blocks = slots // LANES
    highs = cols // LOW
    gx = lax.axis_index("gx")
    strip = lax.axis_index("gy") * gz_count + lax.axis_index("gz")
    has = (gx > 0, gx < gx_count - 1, strip > 0, strip < owners - 1)

    loads = [
        pltpu.make_async_copy(there, here, in_sems.at[i])
        for i, (there, here) in enumerate(
            (
                (pipe_temp_hbm, pipe_temp),
                (contact_hbm, contact),
                (board_hbm, x.at[pl.ds(1, layers)]),
                (coeff_hbm, coeff),
                (pipe_target_hbm, pipe_target),
                (source_hbm, source),
                (target_hbm, target),
            )
        )
    ]
    for load in loads:
        load.start()

    def at_strip(other):
        return {"gy": other // gz_count, "gz": lax.rem(other, gz_count)}

    gx_near = ({"gx": gx - 1}, {"gx": gx + 1})
    strip_near = (at_strip(strip - 1), at_strip(strip + 1))

    barrier = pltpu.get_barrier_semaphore()
    for side in range(2):

        @pl.when(has[side])
        def _():
            pl.semaphore_signal(barrier, inc=1, device_id=gx_near[side], device_id_type=MESH)

    for d in range(1, owners):
        pl.semaphore_signal(
            barrier, inc=1, device_id=at_strip(lax.rem(strip + d, owners)), device_id_type=MESH
        )

    def halo_copy(send, recv, sems, moment, side, near):
        return pltpu.make_async_remote_copy(
            src_ref=send.at[moment, side],
            dst_ref=recv.at[moment, 1 - side],
            send_sem=sems.at[0, moment, side],
            recv_sem=sems.at[1, moment, 1 - side],
            device_id=near[side],
            device_id_type=MESH,
        )

    def arrival(send, recv, sems, moment, side, near):
        return pltpu.make_async_remote_copy(
            src_ref=send.at[moment, side],
            dst_ref=recv.at[moment, side],
            send_sem=sems.at[0, moment, side],
            recv_sem=sems.at[1, moment, side],
            device_id=near[side],
            device_id_type=MESH,
        )

    board_kinds = (
        (row_send, row_recv, row_sems, gx_near, 0),
        (col_send, col_recv, col_sems, strip_near, 2),
    )
    end_kind = ((end_send, end_recv, end_sems, gx_near, 0),)

    def start(kinds, moment):
        for send, recv, sems, near, base in kinds:
            for side in range(2):

                @pl.when(has[base + side])
                def _():
                    halo_copy(send, recv, sems, moment, side, near).start()

    def await_halo(kinds, moment):
        for send, recv, sems, near, base in kinds:
            for side in range(2):

                @pl.when(has[base + side])
                def _():
                    arrival(send, recv, sems, moment, side, near).wait_recv()

    def await_sent(kinds, moment):
        for send, recv, sems, near, base in kinds:
            for side in range(2):

                @pl.when(has[base + side])
                def _():
                    halo_copy(send, recv, sems, moment, side, near).wait_send()

    for send, recv, sems, near, base in board_kinds:
        for side in range(2):

            @pl.when(jnp.logical_not(has[base + side]))
            def _():
                for moment in range(4):
                    recv[moment, side] = jnp.zeros(recv.shape[2:], F32)

    lane_cols = lax.broadcasted_iota(jnp.int32, (rows, cols), 1)
    row_ids = lax.broadcasted_iota(jnp.int32, (rows, cols), 0)
    lane_one = lax.broadcasted_iota(jnp.int32, (rows, LANES), 1)
    end_rows = lax.broadcasted_iota(jnp.int32, (rows, slots), 0)

    def over_layers(body, carry, together):
        together = math.gcd(layers, together)

        def several(step, inner):
            for part in range(together):
                inner = body(step * together + part, inner)
            return inner

        return lax.fori_loop(0, layers // together, several, carry)

    def boundary(field, moment):
        def body(layer, carry):
            low, high = carry
            now = field[layer + 1]
            row_send[moment, 0, pl.ds(layer, 1), :] = now[0:1, :]
            row_send[moment, 1, pl.ds(layer, 1), :] = now[rows - 1 : rows, :]
            mine = lane_one == layer
            low = jnp.where(mine, now[:, 0:1], low)
            high = jnp.where(mine, now[:, cols - 1 : cols], high)
            return low, high

        zero = jnp.zeros((rows, LANES), F32)
        low, high = over_layers(body, (zero, zero), 8)
        col_send[moment, 0] = low
        col_send[moment, 1] = high
        start(board_kinds, moment)

    def laplacian(field, moment, put):
        def body(layer, _):
            now = field[layer + 1]
            above = row_recv[moment, 0, pl.ds(layer, 1), :]
            below = row_recv[moment, 1, pl.ds(layer, 1), :]
            before = pltpu.roll(col_recv[moment, 0], lax.rem(LANES - layer, LANES), 1)
            after = pltpu.roll(col_recv[moment, 1], LANES - 1 - layer, 1)
            if cols > LANES:
                before = jnp.concatenate([before, now[:, LANES:]], axis=1)
                after = jnp.concatenate([now[:, : cols - LANES], after], axis=1)
            up = jnp.where(row_ids == 0, above, pltpu.roll(now, 1, 0))
            down = jnp.where(row_ids == rows - 1, below, pltpu.roll(now, rows - 1, 0))
            left = jnp.where(lane_cols == 0, before, pltpu.roll(now, 1, 1))
            right = jnp.where(lane_cols == cols - 1, after, pltpu.roll(now, cols - 1, 1))
            put(layer, now, (up + down + left + right + field[layer] + field[layer + 2]) - 6.0 * now)
            return 0

        over_layers(body, 0, 4)

    zero_layer = jnp.zeros((rows, cols), F32)
    for field in (x, y, e):
        field[0] = zero_layer
        field[layers + 1] = zero_layer
    sums[...] = jnp.zeros(sums.shape, F32)

    own = owner[...]
    strips = -(-owners // 8) * 8
    strip_ids = lax.broadcasted_iota(jnp.int32, (strips, pipe_count), 0)
    hot = jnp.where(strip_ids == own, 1.0, 0.0).astype(F32)
    earlier = jnp.where(
        lax.broadcasted_iota(jnp.int32, (pipe_count, pipe_count), 0)
        < lax.broadcasted_iota(jnp.int32, (pipe_count, pipe_count), 1),
        1.0,
        0.0,
    ).astype(F32)
    ahead = jnp.dot(hot, earlier, preferred_element_type=F32)
    rank = jnp.sum(hot * ahead, axis=0, keepdims=True)
    place = own * SLOTS + rank.astype(jnp.int32)
    slot_ids = lax.broadcasted_iota(jnp.int32, (slots, pipe_count), 0)
    perm[...] = jnp.where(slot_ids == place, 1.0, 0.0).astype(F32)

    def sort(values):
        return jnp.dot(perm[...], values, precision=EXACT, preferred_element_type=F32)

    near_count = jnp.int32(owners - 1)
    near_count = near_count + jnp.where(has[0], 1, 0) + jnp.where(has[1], 1, 0)
    pl.semaphore_wait(barrier, near_count)

    def exchange(send, recv, which):
        made = []
        for d in range(1, owners):
            other = lax.rem(strip + d, owners)
            made.append(
                pltpu.make_async_remote_copy(
                    src_ref=send.at[pl.ds(pl.multiple_of(other * SLOTS, SLOTS), SLOTS)],
                    dst_ref=recv.at[pl.ds(pl.multiple_of(strip * SLOTS, SLOTS), SLOTS)],
                    send_sem=pipe_sems.at[0, which, d],
                    recv_sem=pipe_sems.at[1, which, d],
                    device_id=at_strip(other),
                    device_id_type=MESH,
                )
            )
        for copy in made:
            copy.start()
        here = pl.ds(pl.multiple_of(strip * SLOTS, SLOTS), SLOTS)
        recv[here, :] = send[here, :]
        return made

    def await_pipes(recv, send, which):
        for d in range(1, owners):
            source_strip = lax.rem(strip + owners - d, owners)
            pltpu.make_async_remote_copy(
                src_ref=send.at[pl.ds(pl.multiple_of(source_strip * SLOTS, SLOTS), SLOTS)],
                dst_ref=recv.at[pl.ds(pl.multiple_of(source_strip * SLOTS, SLOTS), SLOTS)],
                send_sem=pipe_sems.at[0, which, d],
                recv_sem=pipe_sems.at[1, which, d],
                device_id=at_strip(source_strip),
                device_id_type=MESH,
            ).wait_recv()

    loads[0].wait()
    send_a[0] = sort(pipe_temp[...])
    copies = exchange(send_a.at[0], recv_a.at[0], 0)
    loads[1].wait()
    send_a[1] = jnp.dot(perm[...], contact[...].astype(F32), preferred_element_type=F32)
    copies += exchange(send_a.at[1], recv_a.at[1], 1)
    trait_rows = jnp.concatenate(
        [gains[...], conds[...], jnp.zeros((6, pipe_count), F32)], axis=0
    )
    trait_send[...] = lax.dot_general(
        trait_rows,
        perm[...],
        (((1,), (1,)), ((), ())),
        precision=EXACT,
        preferred_element_type=F32,
    )
    trait_copies = []
    for d in range(1, owners):
        trait_copies.append(
            pltpu.make_async_remote_copy(
                src_ref=trait_send,
                dst_ref=trait_recv.at[strip],
                send_sem=pipe_sems.at[0, 4, d],
                recv_sem=pipe_sems.at[1, 4, d],
                device_id=at_strip(lax.rem(strip + d, owners)),
                device_id_type=MESH,
            )
        )
    for copy in trait_copies:
        copy.start()
    copies += trait_copies
    trait_recv[strip] = trait_send[...]
    loads[2].wait()
    boundary(x, 0)
    loads[4].wait()
    send_b[...] = sort(pipe_target[...])
    copies += exchange(send_b, recv_b, 2)
    loads[3].wait()

    def forward_put(to):
        def put(layer, now, lap):
            to[layer + 1] = now + coeff[layer] * lap

        return put

    await_halo(board_kinds, 0)
    laplacian(x, 0, forward_put(y))

    def turn(recv, put):
        for b in range(blocks):
            turned[...] = recv[b * LANES : (b + 1) * LANES, :].T
            for k in range(per_row):
                if per_row == 1:
                    values = turned[...]
                else:
                    values = turned[pl.ds(k, rows, stride=per_row), :]
                put(k, b, values)

    def put_pipes(k, b, values):
        pipes[k, :, b * LANES : (b + 1) * LANES] = values

    def put_wanted(k, b, values):
        wanted[k, :, b * LANES : (b + 1) * LANES] = values

    def put_column(k, b, values):
        column[k, :, b * LANES : (b + 1) * LANES] = values.astype(jnp.int32)

    await_pipes(recv_a.at[0], send_a.at[0], 0)
    turn(recv_a.at[0], put_pipes)

    def send_ends(moment):
        first = pipes[0, 0:8, :]
        last = pipes[per_row - 1, rows - 8 : rows, :]
        end_send[moment, 0] = first
        end_send[moment, 1] = last
        start(end_kind, moment)

    send_ends(0)
    await_pipes(recv_a.at[1], send_a.at[1], 1)
    turn(recv_a.at[1], put_column)
    for d in range(1, owners):
        source_strip = lax.rem(strip + owners - d, owners)
        pltpu.make_async_remote_copy(
            src_ref=trait_send,
            dst_ref=trait_recv.at[source_strip],
            send_sem=pipe_sems.at[0, 4, d],
            recv_sem=pipe_sems.at[1, 4, d],
            device_id=at_strip(source_strip),
            device_id_type=MESH,
        ).wait_recv()
    trait_lane = lax.broadcasted_iota(jnp.int32, (8, slots), 1)
    trait_rows = jnp.zeros((8, slots), F32)
    for other in range(owners):
        shift = lax.rem((other + owners - strip) * SLOTS, slots)
        mine = (trait_lane >= other * SLOTS) & (trait_lane < (other + 1) * SLOTS)
        trait_rows = jnp.where(mine, pltpu.roll(trait_recv[other], shift, 1), trait_rows)
    gain = trait_rows[0:1, :]
    conduct = trait_rows[1:2, :]

    low_ids = lax.broadcasted_iota(jnp.int32, (LOW, slots), 0)
    high_ids = lax.broadcasted_iota(jnp.int32, (highs, slots), 0)

    def hot_body(row, _):
        for k in range(per_row):
            cell = jnp.bitwise_and(column[k, pl.ds(row, 1), :], LOW - 1)
            cells_hot[row, :, k * slots : (k + 1) * slots] = jnp.where(
                low_ids == cell, 1.0, 0.0
            ).astype(jnp.bfloat16)
        return 0

    lax.fori_loop(0, rows, hot_body, 0)

    def spread():
        high_part[...] = flux[...].astype(jnp.bfloat16).astype(F32)
        low_part[...] = flux[...] - high_part[...]

        together = math.gcd(rows, 8)

        def one_row(row):
            parts = []
            for k in range(per_row):
                mine = high_ids == jnp.right_shift(column[k, pl.ds(row, 1), :], 4)
                top = jnp.where(mine, high_part[k, pl.ds(row, 1), :], 0.0)
                rest = jnp.where(mine, low_part[k, pl.ds(row, 1), :], 0.0)
                parts.append(jnp.concatenate([top, rest], axis=0).astype(jnp.bfloat16))
            hot_values = jnp.concatenate(parts, axis=1)
            both = lax.dot_general(
                hot_values,
                cells_hot[row],
                (((1,), (1,)), ((), ())),
                preferred_element_type=F32,
            )
            sums[pl.ds(pl.multiple_of(row * highs, highs), highs), 0:LOW] = both[:highs] + both[highs:]

        def body(step, _):
            for part in range(together):
                one_row(step * together + part)
            return 0

        lax.fori_loop(0, rows // together, body, 0)
        pieces = []
        per_lane = LANES // LOW
        for half in range(cols // LANES):
            total = sums[pl.ds(half * per_lane, rows, stride=highs), :]
            for h in range(1, per_lane):
                total = total + pltpu.roll(
                    sums[pl.ds(half * per_lane + h, rows, stride=highs), :], h * LOW, 1
                )
            pieces.append(total)
        return jnp.concatenate(pieces, axis=1) if len(pieces) > 1 else pieces[0]

    def fetch(field, k):
        out = []
        for b in range(blocks):
            cell = column[k, :, b * LANES : (b + 1) * LANES]
            within = jnp.bitwise_and(cell, LANES - 1)
            which = jnp.right_shift(cell, 7)
            found = None
            for half in range(cols // LANES):
                table = field[1, :, half * LANES : (half + 1) * LANES]
                values = jnp.take_along_axis(table, within, axis=1, mode="promise_in_bounds")
                found = values if found is None else jnp.where(which == half, values, found)
            out.append(found)
        return jnp.concatenate(out, axis=1) if blocks > 1 else out[0]

    def chain_next(moment, sign):
        await_halo(end_kind, moment)
        planes = [pipes[k] for k in range(per_row)]
        first, last = planes[0], planes[-1]
        low = jnp.where(has[0], end_recv[moment, 0, 7:8, :], first[0:1, :])
        high = jnp.where(has[1], end_recv[moment, 1, 0:1, :], last[rows - 1 : rows, :])
        previous = jnp.where(end_rows == 0, low, pltpu.roll(last, 1, 0))
        following = jnp.where(end_rows == rows - 1, high, pltpu.roll(first, rows - 1, 0))
        for k in range(per_row):
            now = planes[k]
            left = planes[k - 1] if k > 0 else previous
            right = planes[k + 1] if k < per_row - 1 else following
            pipes[k] = now + conduct * ((right - now) + (left - now)) + sign * flux[k]

    def couple(field, moment):
        for k in range(per_row):
            apart = pipes[k] - fetch(field, k)
            differ[moment, k] = apart
            flux[k] = gain * (apart + CUBIC_TERM * apart * apart * apart)

    def couple_back(field, moment):
        for k in range(per_row):
            apart = differ[moment, k]
            weight = gain * (1.0 + 3.0 * CUBIC_TERM * apart * apart)
            flux[k] = (BOARD_SHARE * fetch(field, k) - pipes[k]) * weight

    couple(x, 0)
    chain_next(0, -1.0)
    send_ends(1)
    loads[5].wait()
    y[1] = y[1] + powers[0:1, :] * source[...] + BOARD_SHARE * spread()
    boundary(y, 1)

    couple(y, 1)
    chain_next(1, -1.0)
    await_pipes(recv_b, send_b, 2)
    turn(recv_b, put_wanted)
    for k in range(per_row):
        pipes[k] = pipes[k] - wanted[k]
    send_ends(2)
    deposit = spread()
    await_halo(board_kinds, 1)
    loads[6].wait()

    def seed_put(layer, now, lap):
        x[layer + 1] = now + coeff[layer] * lap - target[layer]

    laplacian(y, 1, seed_put)
    x[1] = x[1] + powers[1:2, :] * source[...] + BOARD_SHARE * deposit
    grad_out[...] = powers[1:2, :] * x[1]

    def weigh(layer, _):
        e[layer + 1] = coeff[layer] * x[layer + 1]
        return 0

    over_layers(weigh, 0, 4)
    boundary(e, 2)

    couple_back(x, 1)
    chain_next(2, 1.0)
    send_ends(3)
    deposit = spread()
    await_halo(board_kinds, 2)

    def back_put(layer, now, lap):
        y[layer + 1] = x[layer + 1] + lap

    laplacian(e, 2, back_put)
    y[1] = y[1] - deposit
    grad_out[...] = grad_out[...] + powers[0:1, :] * y[1]

    def weigh_again(layer, _):
        e[layer + 1] = coeff[layer] * y[layer + 1]
        return 0

    over_layers(weigh_again, 0, 4)
    boundary(e, 3)

    couple_back(y, 0)
    chain_next(3, 1.0)
    for b in range(blocks):
        for k in range(per_row):
            values = pipes[k, :, b * LANES : (b + 1) * LANES]
            if per_row == 1:
                turned[...] = values
            else:
                turned[pl.ds(k, rows, stride=per_row), :] = values
        send_c[b * LANES : (b + 1) * LANES, :] = turned[...].T
    copies += exchange(send_c, recv_c, 3)
    deposit = spread()
    await_halo(board_kinds, 3)

    def last_put(layer, now, lap):
        board_out[layer] = y[layer + 1] + lap

    laplacian(e, 3, last_put)
    board_out[0] = board_out[0] - deposit
    await_pipes(recv_c, send_c, 3)
    pipe_out[...] = lax.dot_general(
        perm[...],
        recv_c[...],
        (((0,), (0,)), ((), ())),
        precision=EXACT,
        preferred_element_type=F32,
    )

    for moment in range(4):
        await_sent(board_kinds, moment)
        await_sent(end_kind, moment)
    for copy in copies:
        copy.wait_send()


def solution(mesh):
    gx_count = mesh.shape["gx"]
    gz_count = mesh.shape["gz"]
    owners = mesh.shape["gy"] * gz_count

    def local(
        board_temp,
        board_coeff,
        source,
        board_target,
        pipe_temp,
        pipe_target,
        pipe_cond,
        contact_gain,
        contact_col,
        pipe_owner,
        step_index,
    ):
        layers, rows, cols = board_temp.shape
        pipe_count, nodes = pipe_temp.shape
        per_row = nodes // rows
        slots = owners * SLOTS
        highs = cols // LOW
        moments = step_index[0] + jnp.arange(2, dtype=jnp.int32)
        powers = jnp.broadcast_to(power(moments)[:, None], (2, cols))
        field = pltpu.VMEM((layers + 2, rows, cols), F32)
        planes = pltpu.VMEM((per_row, rows, slots), F32)
        vmem = pl.BlockSpec(memory_space=pltpu.VMEM)
        hbm = pl.BlockSpec(memory_space=pltpu.HBM)
        return pl.pallas_call(
            functools.partial(kernel, (gx_count, gz_count, owners)),
            out_shape=(
                jax.ShapeDtypeStruct(board_temp.shape, F32),
                jax.ShapeDtypeStruct(pipe_temp.shape, F32),
                jax.ShapeDtypeStruct(source.shape, F32),
            ),
            in_specs=[hbm] * 7 + [vmem] * 4,
            out_specs=[vmem] * 3,
            scratch_shapes=[
                pltpu.VMEM(board_coeff.shape, F32),
                pltpu.VMEM(source.shape, F32),
                pltpu.VMEM(board_target.shape, F32),
                pltpu.VMEM(pipe_temp.shape, F32),
                pltpu.VMEM(pipe_target.shape, F32),
                pltpu.VMEM(contact_col.shape, jnp.int32),
                pltpu.SemaphoreType.DMA((7,)),
                pltpu.VMEM((8, slots), F32),
                pltpu.VMEM((owners, 8, slots), F32),
                field,
                field,
                field,
                pltpu.VMEM((slots, pipe_count), F32),
                pltpu.VMEM((2, slots, nodes), F32),
                pltpu.VMEM((slots, nodes), F32),
                pltpu.VMEM((2, slots, nodes), F32),
                pltpu.VMEM((slots, nodes), F32),
                pltpu.VMEM((slots, nodes), F32),
                pltpu.VMEM((slots, nodes), F32),
                pltpu.VMEM((nodes, LANES), F32),
                planes,
                planes,
                planes,
                planes,
                planes,
                pltpu.VMEM((per_row, rows, slots), jnp.int32),
                pltpu.VMEM((rows, LOW, per_row * slots), jnp.bfloat16),
                pltpu.VMEM((2, per_row, rows, slots), F32),
                pltpu.VMEM((rows * highs, LANES), F32),
                pltpu.VMEM((4, 2, layers, cols), F32),
                pltpu.VMEM((4, 2, layers, cols), F32),
                pltpu.VMEM((4, 2, rows, LANES), F32),
                pltpu.VMEM((4, 2, rows, LANES), F32),
                pltpu.VMEM((4, 2, 8, slots), F32),
                pltpu.VMEM((4, 2, 8, slots), F32),
                pltpu.SemaphoreType.DMA((2, 5, owners)),
                pltpu.SemaphoreType.DMA((2, 4, 2)),
                pltpu.SemaphoreType.DMA((2, 4, 2)),
                pltpu.SemaphoreType.DMA((2, 4, 2)),
            ],
            compiler_params=pltpu.CompilerParams(
                collective_id=0, has_side_effects=True, vmem_limit_bytes=48 * 1024 * 1024
            ),
        )(
            board_temp,
            board_coeff,
            source,
            board_target,
            pipe_temp,
            pipe_target,
            contact_col,
            pipe_owner[None, :],
            contact_gain[None, :],
            pipe_cond[None, :],
            powers,
        )

    placed = (
        P("group", "gx", ("gy", "gz")),
        P("group", "gx", ("gy", "gz")),
        P(("group", "gx"), ("gy", "gz")),
        P("group", "gx", ("gy", "gz")),
        P(("group", "gy", "gz"), "gx"),
        P(("group", "gy", "gz"), "gx"),
        P(("group", "gy", "gz")),
        P(("group", "gy", "gz")),
        P(("group", "gy", "gz"), "gx"),
        P(("group", "gy", "gz")),
        P("group"),
    )
    return jax.shard_map(
        local,
        mesh=mesh,
        in_specs=placed,
        out_specs=(
            P("group", "gx", ("gy", "gz")),
            P(("group", "gy", "gz"), "gx"),
            P(("group", "gx"), ("gy", "gz")),
        ),
        check_vma=False,
    )
```
